1024 devices in a mesh: wide: 64 (over z_hi, x, y, core), narrow: 16 (over z_lo).
Axes of the slice: x: 4, y: 4, z: 32 (z_hi: 2, z_lo: 16; z = z_hi * 16 + z_lo), core: 2. Of those that a mesh axis runs over, the one named last changes fastest.
Arguments:
- state: bfloat16 [262144, 128], P(('wide', 'narrow')), may hold values from 0.0099487305 to 1
- block_values: bfloat16 [512, 16, 128, 128], P('wide', 'narrow'), may hold values from 0.00019454956 to 0.0078125
- block_rows: int32 [512, 16], P('wide', 'narrow'), may hold values from 0 to 31
- block_cols: int32 [512, 16], P('wide', 'narrow'), may hold values from 0 to 127
- anchor_ids: int32 [8192], P(('wide', 'narrow')), may hold values from 0 to 262143, as said below
- anchor_class: int32 [8192], P(('wide', 'narrow')), may hold values from 0 to 127
Outputs:
- labels_out: bfloat16 [262144, 128], P(('wide', 'narrow'))
The draws below stay inside these ranges and needn't reach their ends.
Inputs may be any that keep to these rules, and one draw needn't show every extreme that they name: The 8 ids of each aligned block of anchor_ids are distinct documents among the 256 rows of that block's device, in order of devices.
All inputs are finite; a program needn't handle non-finite values.
Results may differ from the reference program's by a relative error of at most 0.0045.
Values may be sent and summed in bfloat16 or wider, within the bound.
No kernel may reach another device: no remote copies, remote signals or barrier semaphores. Data moves between devices by JAX's collectives and lax.ppermute only.
A program may use at most 32 MiB of HBM per device.

```python
import math
import jax
import jax.numpy as jnp
import numpy as np
from jax import lax

BLOCK = 128
LABELS = 128
ROW_DEG = 4
DOC_DEV = 256
ANC_DEV = 8
ITERS = 1
NNZ_DEV = 8
GROUP_BLOCKS = 128
PANEL_BLOCKS = 32
DOCS = 262144
ANCHORS = 8192
N_WIDE = 64
N_NARROW = 16
DEVICES = 1024


def draw_anchor_ids(key, part):
    key = jax.random.fold_in(key, 11)
    keys = jax.random.split(key, DEVICES)

    def pick_rows(single):
        return jax.random.permutation(single, DOC_DEV)[:ANC_DEV].astype(jnp.int32)
    picks = jax.vmap(pick_rows)(keys)
    offsets = jnp.arange(DEVICES, dtype=jnp.int32)[:, None] * DOC_DEV
    return (picks + offsets).reshape(-1)


def place_ends(array, own_key, low, largest):
    spot = [jax.random.randint(jax.random.fold_in(own_key, axis), (), 0, length) for axis, length in enumerate(array.shape)]
    longest = array.shape.index(max(array.shape))
    neighbour = spot[:longest] + [(spot[longest] + 1) % array.shape[longest]] + spot[longest + 1:]
    return array.at[tuple(spot)].set(low).at[tuple(neighbour)].set(largest)


def level_of(own_key, dims, pieces, smallest, high):
    def one(axis_at, blocks):
        draws = jax.random.uniform(jax.random.fold_in(jax.random.fold_in(own_key, 6), axis_at), (blocks,), jnp.float32, smallest / len(pieces), high / len(pieces))
        return jnp.repeat(jnp.exp(draws), dims[axis_at] // blocks).reshape((-1,) + (1,) * (len(dims) - axis_at - 1))

    gain = one(*pieces[0])
    for cut in pieces[1:]:
        gain = gain * one(*cut)
    return gain


def cumulative_ranks(count, skew):
    weights = [(1 << 20) // math.isqrt(standing ** skew) + 1 for standing in range(1, count + 1)]
    scale = 1 + sum(weights) // (1 << 30)
    return np.cumsum(np.array([max(1, weight // scale) for weight in weights]))


def ranked_ids(rng, shape, count, slope):
    grid = cumulative_ranks(count, slope)
    pick = jax.random.randint(jax.random.fold_in(rng, 1), shape, 0, int(grid[count - 1]))
    grade = jnp.searchsorted(jnp.asarray(grid, jnp.int32), pick, side="right")
    return jax.random.permutation(jax.random.fold_in(rng, 2), count)[grade].astype(jnp.int32)


def setup_inputs(seed: int = 0) -> dict:
    key_list = jax.random.split(jax.random.key(seed), 7)
    return {
        "state": jnp.clip(jnp.exp(math.log(1.0) - 4.61031033 * jax.random.uniform(key_list[0], (DOCS, LABELS), jnp.float32) ** level_of(key_list[0], (DOCS, LABELS), ((0, 1024),), -0.2, 0.2)), 0.0099487305, 1.0).astype(jnp.bfloat16),
        "block_values": jnp.clip(jnp.exp(math.log(0.0078125) - 3.6927934 * jax.random.uniform(key_list[1], (N_WIDE * NNZ_DEV, N_NARROW, BLOCK, BLOCK), jnp.float32) ** level_of(key_list[1], (N_WIDE * NNZ_DEV, N_NARROW, BLOCK, BLOCK), ((0, 64), (1, 16)), -0.2, 0.2)), 0.00019454956, 0.0078125).astype(jnp.bfloat16),
        "block_rows": place_ends(ranked_ids(key_list[2], (N_WIDE * NNZ_DEV, N_NARROW), PANEL_BLOCKS, 2), jax.random.fold_in(key_list[2], 3), 0, PANEL_BLOCKS - 1).astype(jnp.int32),
        "block_cols": place_ends(jax.random.randint(key_list[3], (N_WIDE * NNZ_DEV, N_NARROW), 0, GROUP_BLOCKS), jax.random.fold_in(key_list[3], 1), 0, GROUP_BLOCKS - 1).astype(jnp.int32),
        "anchor_ids": draw_anchor_ids(jax.random.fold_in(key_list[6], 71), 0),
        "anchor_class": place_ends(jax.random.randint(key_list[5], (ANCHORS,), 0, LABELS), jax.random.fold_in(key_list[5], 1), 0, LABELS - 1).astype(jnp.int32),
    }


def reference(state, block_values, block_rows, block_cols, anchor_ids, anchor_class):
    cb = DOC_DEV // BLOCK
    nnz = ROW_DEG * cb
    panel_blocks = N_NARROW * cb
    nidx = jnp.arange(N_NARROW, dtype=jnp.int32)
    values = block_values.reshape(N_WIDE, nnz, N_NARROW, BLOCK, BLOCK)
    owners = block_rows.reshape(N_WIDE, nnz, N_NARROW)
    cols = block_cols.reshape(N_WIDE, nnz, N_NARROW)
    column = ((cols // cb) * N_NARROW + nidx[None, None, :]) * cb + (cols % cb)
    anchored = jnp.zeros((DOCS,), jnp.bool_).at[anchor_ids].set(True)
    fixed = jnp.zeros((DOCS, LABELS), jnp.float32).at[anchor_ids].set(
        jax.nn.one_hot(anchor_class, LABELS, dtype=jnp.float32))
    current = state
    for step in range(ITERS):
        blocks = current.reshape(DOCS // BLOCK, BLOCK, LABELS)

        def panel(triple):
            vals, rows, colw = triple
            gathered = blocks[colw].astype(jnp.float32)
            contrib = jnp.einsum('knrm,knml->knrl', vals.astype(jnp.float32), gathered)
            onehot = jax.nn.one_hot(rows, panel_blocks, dtype=jnp.float32)
            part = jnp.einsum('knb,knrl->nbrl', onehot, contrib)
            part = lax.optimization_barrier(part.astype(jnp.bfloat16)).astype(jnp.float32)
            return jnp.sum(part, axis=0).reshape(panel_blocks * BLOCK, LABELS)

        sums = lax.map(panel, (values, owners, column)).reshape(DOCS, LABELS)
        total = sums + current.astype(jnp.float32)
        spread = total / jnp.sum(total, axis=-1, keepdims=True)
        spread = jnp.where(anchored[:, None], fixed, spread)
        current = spread.astype(jnp.bfloat16)
    return current
```

```python
import functools

import jax
import jax.numpy as jnp
from jax import lax
from jax.experimental import pallas as pl
from jax.experimental.pallas import tpu as pltpu
from jax.sharding import Mesh, PartitionSpec as P

WIDE = ("zh", "x", "y", "c")
PLANE = ("x", "y")
HALF, SIDE, LINE = 2, 4, 16
N_PLANE = SIDE * SIDE


def swap(value, axis):
    return lax.ppermute(value, axis, [(0, 1), (1, 0)])


def exchange(value, step):
    return lax.ppermute(value, "zl", [(i, i ^ step) for i in range(LINE)])


def plane_gather(value):
    spread = jnp.broadcast_to(value[None], (N_PLANE,) + value.shape)
    return lax.all_to_all(spread, PLANE, 0, 0)


def product_kernel(where, index, values, s00, s01, s10, s11, out, picked, sems):
    count = values.shape[0]
    width = values.shape[1]
    for k in range(count):
        for code, source in enumerate((s00, s01, s10, s11)):

            @pl.when(where[k] == code)
            def _():
                start = pl.multiple_of(index[k] * width, width)
                pltpu.make_async_copy(
                    source.at[pl.ds(start, width)], picked.at[k], sems.at[k]
                ).start()

    for k in range(count):
        pltpu.make_async_copy(s00.at[pl.ds(0, width)], picked.at[k], sems.at[k]).wait()
        out[k] = jnp.dot(
            values[k], picked[k], preferred_element_type=jnp.float32
        ).astype(out.dtype)


def products(where, index, values, sources):
    count, width, _ = values.shape
    labels = sources[0].shape[-1]
    smem = pl.BlockSpec(memory_space=pltpu.SMEM)
    vmem = pl.BlockSpec(memory_space=pltpu.VMEM)
    anywhere = pl.BlockSpec(memory_space=pl.ANY)
    return pl.pallas_call(
        product_kernel,
        out_shape=jax.ShapeDtypeStruct((count, width, labels), jnp.bfloat16),
        in_specs=[smem, smem, vmem] + [anywhere] * 4,
        out_specs=vmem,
        scratch_shapes=[
            pltpu.VMEM((count, width, labels), jnp.bfloat16),
            pltpu.SemaphoreType.DMA((count,)),
        ],
        cost_estimate=pl.CostEstimate(
            flops=2 * count * width * width * labels,
            bytes_accessed=6 * count * width * labels,
            transcendentals=0,
        ),
        name="products",
    )(where, index, values, *sources)


def collect_kernel(slot, mine, theirs, out, total):
    count = mine.shape[0]
    slots = out.shape[0]
    total[...] = jnp.zeros_like(total)
    for side, source in enumerate((mine, theirs)):
        for k in range(count):
            place = slot[side * count + k]

            @pl.when(place < slots)
            def _():
                total[place] += source[k].astype(jnp.float32)

    out[...] = total[...].astype(out.dtype)


def collect(slot, mine, theirs, slots):
    count, width, labels = mine.shape
    smem = pl.BlockSpec(memory_space=pltpu.SMEM)
    vmem = pl.BlockSpec(memory_space=pltpu.VMEM)
    return pl.pallas_call(
        collect_kernel,
        out_shape=jax.ShapeDtypeStruct((slots, width, labels), jnp.bfloat16),
        in_specs=[smem, vmem, vmem],
        out_specs=vmem,
        scratch_shapes=[pltpu.VMEM((slots, width, labels), jnp.float32)],
        cost_estimate=pl.CostEstimate(
            flops=2 * count * width * labels,
            bytes_accessed=(4 * count + 2 * slots) * width * labels,
            transcendentals=0,
        ),
        name="collect",
    )(slot, mine, theirs)


def local(state, block_values, block_rows, block_cols, anchor_ids, anchor_class):
    doc_dev, labels = state.shape
    width = block_values.shape[2]
    per_dev = doc_dev // width
    values = block_values[:, 0]
    cols = block_cols[:, 0]
    rows = block_rows[:, 0]
    zh, core, line = (lax.axis_index(a) for a in ("zh", "c", "zl"))
    bits = [(line // s) % 2 for s in (1, 2, 4, 8)]

    far = swap(state, "zh")
    near_own = plane_gather(state).reshape(-1, labels)
    their_rows = exchange(rows, 1)
    far_own = plane_gather(far).reshape(-1, labels)
    near_other = swap(near_own, "c")
    far_other = swap(far_own, "c")

    owner_dev, inner = cols // per_dev, cols % per_dev
    col_core = owner_dev % 2
    col_plane = (owner_dev // 2) % N_PLANE
    col_half = owner_dev // (2 * N_PLANE)
    where = 2 * (col_half != zh).astype(jnp.int32) + (col_core != core).astype(jnp.int32)
    index = col_plane * per_dev + inner
    mine = products(where, index, values, (near_own, near_other, far_own, far_other))

    both = jnp.concatenate([rows, their_rows])
    owner, inner = both // per_dev, both % per_dev
    b = [(owner // s) % 2 for s in (1, 2, 4, 8)]
    slot = ((b[1] * 2 + b[2]) * 2 + b[3]) * per_dev + inner
    slots = LINE // 2 * per_dev
    slot = jnp.where(b[0] == bits[0], slot, slots)
    theirs = exchange(mine, 1)
    held = collect(slot, mine, theirs, slots)
    for step, bit in ((2, bits[1]), (4, bits[2]), (8, bits[3])):
        halves = held.reshape((2, held.shape[0] // 2) + held.shape[1:])
        keep = lax.dynamic_index_in_dim(halves, bit, 0, keepdims=False)
        send = lax.dynamic_index_in_dim(halves, 1 - bit, 0, keepdims=False)
        got = exchange(send, step)
        held = keep.astype(jnp.float32) + got.astype(jnp.float32)
        if step < 8:
            held = held.astype(jnp.bfloat16)
    sums = held.reshape(doc_dev, labels)

    first_row = lax.axis_index(WIDE + ("zl",)) * doc_dev
    local_ids = anchor_ids - first_row
    match = local_ids[:, None] == jnp.arange(doc_dev, dtype=jnp.int32)[None, :]
    match = match.astype(jnp.float32)
    anchored = jnp.sum(match, axis=0) > 0.5
    fixed = jnp.dot(match.T, jax.nn.one_hot(anchor_class, labels, dtype=jnp.float32))
    total = sums + state.astype(jnp.float32)
    spread = total / jnp.sum(total, axis=-1, keepdims=True)
    spread = jnp.where(anchored[:, None], fixed, spread)
    return spread.astype(jnp.bfloat16)


def solution(mesh):
    shape = (HALF, SIDE, SIDE, 2, LINE)
    fine = Mesh(mesh.devices.reshape(shape), WIDE + ("zl",))
    every = WIDE + ("zl",)
    in_specs = (
        P(every, None),
        P(WIDE, "zl", None, None),
        P(WIDE, "zl"),
        P(WIDE, "zl"),
        P(every),
        P(every),
    )
    return jax.shard_map(
        local, mesh=fine, in_specs=in_specs, out_specs=P(every, None), check_vma=False
    )
```

```python
import jax
import jax.numpy as jnp
from jax import lax
from jax.experimental import pallas as pl
from jax.experimental.pallas import tpu as pltpu
from jax.sharding import Mesh, PartitionSpec as P

WIDE = ("zh", "x", "y", "c")
PLANE = ("x", "y")
HALF, SIDE, LINE = 2, 4, 16
N_PLANE = SIDE * SIDE
SMEM = pl.BlockSpec(memory_space=pltpu.SMEM)
VMEM = pl.BlockSpec(memory_space=pltpu.VMEM)


def cost(flops, nbytes):
    return pl.CostEstimate(flops=flops, bytes_accessed=nbytes, transcendentals=0)


def swap(value, axis):
    return lax.ppermute(value, axis, [(0, 1), (1, 0)])


def exchange(value, step):
    return lax.ppermute(value, "zl", [(i, i ^ step) for i in range(LINE)])


def spread(value):
    return jnp.broadcast_to(value[None], (N_PLANE,) + value.shape)


def plane_exchange(value):
    return lax.all_to_all(value, PLANE, 0, 0)


def product_kernel(facts, values, s00, s01, s10, s11, first, second, picked):
    count, width = values.shape[:2]
    half = width // 2
    for k in range(count):
        start = pl.multiple_of(facts[count + k] * width, width)
        for number, source in enumerate((s00, s01, s10, s11)):

            @pl.when(facts[k] == number)
            def _():
                picked[k] = source[pl.ds(start, width), :]

    for k in range(count):
        out = jnp.dot(values[k], picked[k], preferred_element_type=jnp.float32)
        first[k] = out[:half].astype(first.dtype)
        second[k] = out[half:].astype(second.dtype)


def products(facts, values, sources):
    count, width, _ = values.shape
    labels = sources[0].shape[-1]
    part = jax.ShapeDtypeStruct((count, width // 2, labels), jnp.bfloat16)
    return pl.pallas_call(
        product_kernel,
        out_shape=(part, part),
        in_specs=[SMEM] + [VMEM] * 5,
        out_specs=(VMEM, VMEM),
        scratch_shapes=[pltpu.VMEM((count, width, labels), jnp.bfloat16)],
        compiler_params=pltpu.CompilerParams(vmem_limit_bytes=16 * 2**20),
        cost_estimate=cost(2 * count * width * width * labels, 6 * count * width * labels),
        name="products",
    )(facts, values, *sources)


def collect_kernel(slot, mine, theirs, keep, send, total):
    count = mine.shape[0]
    slots = keep.shape[0]
    total[...] = jnp.zeros_like(total)
    for side, source in enumerate((mine, theirs)):
        for k in range(count):
            place = slot[side * count + k]

            @pl.when(place < 2 * slots)
            def _():
                total[place] += source[k].astype(jnp.float32)

    send[...] = total[slots:].astype(send.dtype)
    keep[...] = total[:slots].astype(keep.dtype)


def collect(slot, mine, theirs, slots):
    count, rows, labels = mine.shape
    part = jax.ShapeDtypeStruct((slots, rows, labels), jnp.bfloat16)
    return pl.pallas_call(
        collect_kernel,
        out_shape=(part, part),
        in_specs=[SMEM, VMEM, VMEM],
        out_specs=(VMEM, VMEM),
        scratch_shapes=[pltpu.VMEM((2 * slots, rows, labels), jnp.float32)],
        cost_estimate=cost(2 * count * rows * labels, (4 * count + 4 * slots) * rows * labels),
        name="collect",
    )(slot, mine, theirs)


def local(state, block_values, block_rows, block_cols, anchor_ids, anchor_class):
    doc_dev, labels = state.shape
    width = block_values.shape[2]
    per_dev = doc_dev // width
    values = block_values[:, 0]
    cols = block_cols[:, 0]
    rows = block_rows[:, 0]
    zh, core, line = (lax.axis_index(a) for a in ("zh", "c", "zl"))
    bits = {s: (line // s) % 2 for s in (1, 2, 4, 8)}

    owner_dev, inner = cols // per_dev, cols % per_dev
    col_core = owner_dev % 2
    col_plane = (owner_dev // 2) % N_PLANE
    col_half = owner_dev // (2 * N_PLANE)
    where = 2 * (col_half != zh).astype(jnp.int32) + (col_core != core).astype(jnp.int32)
    facts = jnp.concatenate([where, col_plane * per_dev + inner])

    copies = spread(state)
    from_second = lax.ppermute(state, "zh", [(1, 0)])
    near_own = lax.cond(zh == 0, plane_exchange, lambda value: value, copies)
    again, near_own = lax.optimization_barrier((state, near_own))
    from_first = lax.ppermute(again, "zh", [(0, 1)])
    near_own = lax.cond(zh == 1, plane_exchange, lambda value: value, near_own)
    far = jnp.where(zh == 0, from_second, from_first)
    rows_late, near_own = lax.optimization_barrier((rows, near_own))
    both = jnp.concatenate([rows, exchange(rows_late, 1)])
    owner, inner = both // per_dev, both % per_dev
    b = {s: (owner // s) % 2 for s in (1, 2, 4, 8)}
    slots = LINE // 4 * per_dev
    slot = (b[4] * 2 + b[8]) * per_dev + inner
    slot = slot + jnp.where(b[2] == bits[2], 0, slots)
    slot = jnp.where(b[1] == bits[1], slot, 2 * slots)
    far_own = plane_exchange(spread(far)).reshape(-1, labels)
    far_own, facts, slot = lax.optimization_barrier((far_own, facts, slot))
    near_own = near_own.reshape(-1, labels)
    near_other = swap(near_own, "c")
    far_other = swap(far_own, "c")
    mine = products(facts, values, (near_own, near_other, far_own, far_other))

    theirs = [exchange(part, 1) for part in mine]
    held = [collect(slot, *parts, slots) for parts in zip(mine, theirs)]
    got = [exchange(send, 2) for _, send in held]

    def halve(keep, came, step):
        pair = (2, keep.shape[0] // 2) + keep.shape[1:]
        keep, came = keep.reshape(pair), came.reshape(pair)
        bit = bits[step]

        def side(index):
            one = lax.dynamic_index_in_dim(keep, index, 0, keepdims=False)
            two = lax.dynamic_index_in_dim(came, index, 0, keepdims=False)
            return one + two

        return side(bit), side(1 - bit)

    held = [halve(keep, came, 4) for (keep, _), came in zip(held, got)]
    got = [exchange(send, 4) for _, send in held]
    held = [halve(keep, came, 8) for (keep, _), came in zip(held, got)]
    keep, send = (jnp.concatenate(parts, axis=1) for parts in zip(*held))
    sums = keep.astype(jnp.float32) + exchange(send, 8).astype(jnp.float32)
    sums = sums.reshape(doc_dev, labels)

    first_row = lax.axis_index(WIDE + ("zl",)) * doc_dev
    local_ids = anchor_ids - first_row
    match = local_ids[:, None] == jnp.arange(doc_dev, dtype=jnp.int32)[None, :]
    match = match.astype(jnp.float32)
    anchored = jnp.sum(match, axis=0) > 0.5
    fixed = jnp.dot(match.T, jax.nn.one_hot(anchor_class, labels, dtype=jnp.float32))
    total = sums + state.astype(jnp.float32)
    result = total / jnp.sum(total, axis=-1, keepdims=True)
    result = jnp.where(anchored[:, None], fixed, result)
    return result.astype(jnp.bfloat16)


def solution(mesh):
    shape = (HALF, SIDE, SIDE, 2, LINE)
    every = WIDE + ("zl",)
    fine = Mesh(mesh.devices.reshape(shape), every)
    in_specs = (
        P(every, None),
        P(WIDE, "zl", None, None),
        P(WIDE, "zl"),
        P(WIDE, "zl"),
        P(every),
        P(every),
    )
    return jax.shard_map(
        local, mesh=fine, in_specs=in_specs, out_specs=P(every, None), check_vma=False
    )
```

```python
import functools

import jax
import jax.numpy as jnp
from jax import lax
from jax.experimental import pallas as pl
from jax.experimental.pallas import tpu as pltpu
from jax.sharding import Mesh, PartitionSpec as P

WIDE = ("zh", "x", "y", "c")
PLANE = ("x", "y")
HALF, SIDE, LINE = 2, 4, 16
N_PLANE = SIDE * SIDE
SMEM = pl.BlockSpec(memory_space=pltpu.SMEM)
VMEM = pl.BlockSpec(memory_space=pltpu.VMEM)


def cost(flops, nbytes):
    return pl.CostEstimate(flops=flops, bytes_accessed=nbytes, transcendentals=0)


def swap(value, axis):
    return lax.ppermute(value, axis, [(0, 1), (1, 0)])


def exchange(value, step):
    return lax.ppermute(value, "zl", [(i, i ^ step) for i in range(LINE)])


def spread(value):
    return jnp.broadcast_to(value[None], (N_PLANE,) + value.shape)


def plane_exchange(value):
    return lax.all_to_all(value, PLANE, 0, 0)


def blank_kernel(out):
    pass


def blank(like):
    return pl.pallas_call(
        blank_kernel,
        out_shape=jax.ShapeDtypeStruct((N_PLANE,) + like.shape, like.dtype),
        out_specs=pl.BlockSpec(memory_space=pl.ANY),
        cost_estimate=cost(0, 0),
        name="blank",
    )()


def small(limit):
    return pltpu.CompilerParams(vmem_limit_bytes=limit * 2**20)


def product_kernel(facts, values, s00, s01, s10, s11, first, second, picked):
    count, width = values.shape[:2]
    half = width // 2
    shift = (s00.shape[0] // width // N_PLANE).bit_length() - 1
    zh, mine = lax.axis_index("zh"), lax.axis_index("c")
    for k in range(count):
        col = facts[count + k]
        device, inner = col >> shift, col & ((1 << shift) - 1)
        core, flat, far = device & 1, (device >> 1) & (N_PLANE - 1), (device >> 1) >> 4
        code = 2 * (far ^ zh) + (core ^ mine)
        start = pl.multiple_of(((flat << shift) + inner) * width, width)
        for number, source in enumerate((s00, s01, s10, s11)):

            @pl.when(code == number)
            def _():
                picked[k] = source[pl.ds(start, width), :]

    for k in range(count):
        out = jnp.dot(values[k], picked[k], preferred_element_type=jnp.float32)
        first[k] = out[:half].astype(first.dtype)
        second[k] = out[half:].astype(second.dtype)


def products(facts, values, sources):
    count, width, _ = values.shape
    labels = sources[0].shape[-1]
    part = jax.ShapeDtypeStruct((count, width // 2, labels), jnp.bfloat16)
    return pl.pallas_call(
        product_kernel,
        out_shape=(part, part),
        in_specs=[SMEM] + [VMEM] * 5,
        out_specs=(VMEM, VMEM),
        scratch_shapes=[pltpu.VMEM((count, width, labels), jnp.bfloat16)],
        compiler_params=small(16),
        cost_estimate=cost(2 * count * width * width * labels, 6 * count * width * labels),
        name="products",
    )(facts, values, *sources)


def collect_kernel(per_dev, order, rows, other_rows, mine, theirs, keep, send, total):
    slots = keep.shape[0]
    line = lax.axis_index("zl")
    shift = per_dev.bit_length() - 1
    total[...] = jnp.zeros_like(total)
    for numbers, source in ((rows, mine), (other_rows, theirs)):
        for k in range(source.shape[0]):
            owner, inner = numbers[k] >> shift, numbers[k] & (per_dev - 1)
            pair = ((owner >> 2) & 1) * 2 + (owner >> 3)
            differs = owner ^ line
            goes = (differs >> order[1]) & 1
            place = (pair << shift) + inner + goes * slots

            @pl.when(((differs >> order[0]) & 1) == 0)
            def _():
                total[place] += source[k].astype(jnp.float32)

    send[...] = total[slots:].astype(send.dtype)
    keep[...] = total[:slots].astype(keep.dtype)


def collect(per_dev, order, rows, other_rows, mine, theirs):
    count, height, labels = mine.shape
    slots = LINE // 4 * per_dev
    part = jax.ShapeDtypeStruct((slots, height, labels), jnp.bfloat16)
    return pl.pallas_call(
        functools.partial(collect_kernel, per_dev, order),
        out_shape=(part, part),
        in_specs=[SMEM, SMEM, VMEM, VMEM],
        out_specs=(VMEM, VMEM),
        scratch_shapes=[pltpu.VMEM((2 * slots, height, labels), jnp.float32)],
        compiler_params=small(4),
        cost_estimate=cost(2 * count * height * labels, (4 * count + 4 * slots) * height * labels),
        name="collect",
    )(rows, other_rows, mine, theirs)


def finish_kernel(anchor, first, second, came, state, out, result):
    docs, labels = state.shape
    slots, half = first.shape[:2]
    lane = lax.broadcasted_iota(jnp.int32, (1, labels), 1)
    for slot in range(slots):
        for side, keep in enumerate((first, second)):
            rows = pl.ds(side * half, half)
            here = pl.ds((slot * 2 + side) * half, half)
            total = keep[slot].astype(jnp.float32) + came[slot, rows].astype(jnp.float32)
            total = total + state[here].astype(jnp.float32)
            result[here] = total / jnp.sum(total, axis=-1, keepdims=True)
    count = anchor.shape[0] // 2
    first_row = lax.axis_index(WIDE + ("zl",)) * docs
    for k in range(count):
        row = anchor[k] - first_row
        result[pl.ds(row, 1)] = (lane == anchor[count + k]).astype(jnp.float32)
    out[...] = result[...].astype(out.dtype)


def finish(anchor, keep, came, state):
    docs, labels = state.shape
    return pl.pallas_call(
        finish_kernel,
        out_shape=jax.ShapeDtypeStruct(state.shape, state.dtype),
        in_specs=[SMEM] + [VMEM] * 4,
        out_specs=VMEM,
        scratch_shapes=[pltpu.VMEM((docs, labels), jnp.float32)],
        compiler_params=small(4),
        cost_estimate=cost(6 * docs * labels, 10 * docs * labels),
        name="finish",
    )(anchor, *keep, came, state)


def local(state, block_values, block_rows, block_cols, anchor_ids, anchor_class):
    doc_dev, labels = state.shape
    width = block_values.shape[2]
    per_dev = doc_dev // width
    values = block_values[:, 0]
    cols = block_cols[:, 0]
    rows = block_rows[:, 0]
    zh, line = lax.axis_index("zh"), lax.axis_index("zl")
    bits = {s: (line >> b) & 1 for b, s in enumerate((1, 2, 4, 8))}

    from_second = lax.ppermute(state, "zh", [(1, 0)])

    def fill(index, buffer, value):
        def gather(buffer, value):
            return plane_exchange(spread(value))

        return lax.cond(zh == index, gather, lambda buffer, value: buffer, buffer, value)

    near_own = fill(0, blank(state), state)
    again, near_own = lax.optimization_barrier((state, near_own))
    from_first = lax.ppermute(again, "zh", [(0, 1)])
    near_own, from_second = lax.optimization_barrier((near_own, from_second))
    near_own = fill(1, near_own, state)
    far = jnp.where(zh == 0, from_second, from_first)
    facts, near_own = lax.optimization_barrier((jnp.concatenate([rows, cols]), near_own))
    other_facts = tuple(exchange(facts, step) for step in (1, 2))
    far_own = plane_exchange(spread(far)).reshape(-1, labels)
    far_own, other_facts = lax.optimization_barrier((far_own, other_facts))
    near_own = near_own.reshape(-1, labels)
    near_other = swap(near_own, "c")
    far_other = swap(far_own, "c")
    mine = products(facts, values, (near_own, near_other, far_own, far_other))

    theirs = [exchange(part, step) for part, step in zip(mine, (1, 2))]
    held = [
        collect(per_dev, order, facts, *parts)
        for order, *parts in zip(((0, 1), (1, 0)), other_facts, mine, theirs)
    ]
    got = [exchange(send, step) for (_, send), step in zip(held, (2, 1))]

    def halve(keep, came, step):
        pair = (2, keep.shape[0] // 2) + keep.shape[1:]
        keep, came = keep.reshape(pair), came.reshape(pair)
        bit = bits[step]

        def at(value, index):
            starts, sizes = (index,) + (0,) * 3, (1,) + value.shape[1:]
            return lax.dynamic_slice(value, starts, sizes, allow_negative_indices=False)[0]

        def side(index):
            one = at(keep, index)
            two = at(came, index)
            return one + two

        return side(bit), side(1 - bit)

    held = [halve(keep, came, 4) for (keep, _), came in zip(held, got)]
    got = [exchange(send, 4) for _, send in held]
    held = [halve(keep, came, 8) for (keep, _), came in zip(held, got)]
    send = jnp.concatenate([send for _, send in held], axis=1)
    anchor = lax.optimization_barrier(jnp.concatenate([anchor_ids, anchor_class]))
    return finish(anchor, [keep for keep, _ in held], exchange(send, 8), state)


def solution(mesh):
    shape = (HALF, SIDE, SIDE, 2, LINE)
    every = WIDE + ("zl",)
    fine = Mesh(mesh.devices.reshape(shape), every)
    in_specs = (
        P(every, None),
        P(WIDE, "zl", None, None),
        P(WIDE, "zl"),
        P(WIDE, "zl"),
        P(every),
        P(every),
    )
    return jax.shard_map(
        local, mesh=fine, in_specs=in_specs, out_specs=P(every, None), check_vma=False
    )
```

```python
import functools

import jax
import jax.numpy as jnp
from jax import lax
from jax.experimental import pallas as pl
from jax.experimental.pallas import tpu as pltpu
from jax.sharding import Mesh, PartitionSpec as P

WIDE = ("zh", "x", "y", "c")
PLANE = ("x", "y")
HALF, SIDE, LINE = 2, 4, 16
N_PLANE = SIDE * SIDE
SMEM = pl.BlockSpec(memory_space=pltpu.SMEM)
VMEM = pl.BlockSpec(memory_space=pltpu.VMEM)


def cost(flops, nbytes):
    return pl.CostEstimate(flops=flops, bytes_accessed=nbytes, transcendentals=0)


def swap(value, axis):
    return lax.ppermute(value, axis, [(0, 1), (1, 0)])


def exchange(value, step):
    return lax.ppermute(value, "zl", [(i, i ^ step) for i in range(LINE)])


def spread(value):
    return jnp.broadcast_to(value[None], (N_PLANE,) + value.shape)


def plane_exchange(value):
    return lax.all_to_all(value, PLANE, 0, 0)


def blank_kernel(out):
    pass


def blank(like):
    return pl.pallas_call(
        blank_kernel,
        out_shape=jax.ShapeDtypeStruct((N_PLANE,) + like.shape, like.dtype),
        out_specs=pl.BlockSpec(memory_space=pl.ANY),
        cost_estimate=cost(0, 0),
        name="blank",
    )()


def small(limit):
    return pltpu.CompilerParams(vmem_limit_bytes=limit * 2**20)


def product_kernel(facts, values, s00, s01, s10, s11, first, second, picked):
    count, width = values.shape[:2]
    half = width // 2
    shift = (s00.shape[0] // width // N_PLANE).bit_length() - 1
    zh, mine = lax.axis_index("zh"), lax.axis_index("c")
    for k in range(count):
        col = facts[count + k]
        device, inner = col >> shift, col & ((1 << shift) - 1)
        core, flat, far = device & 1, (device >> 1) & (N_PLANE - 1), (device >> 1) >> 4
        code = 2 * (far ^ zh) + (core ^ mine)
        start = pl.multiple_of(((flat << shift) + inner) * width, width)
        for number, source in enumerate((s00, s01, s10, s11)):

            @pl.when(code == number)
            def _():
                picked[k] = source[pl.ds(start, width), :]

    for k in range(count):
        out = jnp.dot(values[k], picked[k], preferred_element_type=jnp.float32)
        first[k] = out[:half].astype(first.dtype)
        second[k] = out[half:].astype(second.dtype)


def products(facts, values, sources):
    count, width, _ = values.shape
    labels = sources[0].shape[-1]
    part = jax.ShapeDtypeStruct((count, width // 2, labels), jnp.bfloat16)
    return pl.pallas_call(
        product_kernel,
        out_shape=(part, part),
        in_specs=[SMEM] + [VMEM] * 5,
        out_specs=(VMEM, VMEM),
        scratch_shapes=[pltpu.VMEM((count, width, labels), jnp.bfloat16)],
        compiler_params=small(16),
        cost_estimate=cost(2 * count * width * width * labels, 6 * count * width * labels),
        name="products",
    )(facts, values, *sources)


def collect_kernel(per_dev, order, rows, other_rows, mine, theirs, keep, send, total):
    slots = keep.shape[0]
    line = lax.axis_index("zl")
    shift = per_dev.bit_length() - 1
    total[...] = jnp.zeros_like(total)
    for numbers, source in ((rows, mine), (other_rows, theirs)):
        for k in range(source.shape[0]):
            owner, inner = numbers[k] >> shift, numbers[k] & (per_dev - 1)
            pair = ((owner >> 2) & 1) * 2 + (owner >> 3)
            differs = owner ^ line
            goes = (differs >> order[1]) & 1
            place = (pair << shift) + inner + goes * slots

            @pl.when(((differs >> order[0]) & 1) == 0)
            def _():
                total[place] += source[k].astype(jnp.float32)

    send[...] = total[slots:].astype(send.dtype)
    keep[...] = total[:slots].astype(keep.dtype)


def collect(per_dev, order, rows, other_rows, mine, theirs):
    count, height, labels = mine.shape
    slots = LINE // 4 * per_dev
    part = jax.ShapeDtypeStruct((slots, height, labels), jnp.bfloat16)
    return pl.pallas_call(
        functools.partial(collect_kernel, per_dev, order),
        out_shape=(part, part),
        in_specs=[SMEM, SMEM, VMEM, VMEM],
        out_specs=(VMEM, VMEM),
        scratch_shapes=[pltpu.VMEM((2 * slots, height, labels), jnp.float32)],
        compiler_params=small(4),
        cost_estimate=cost(2 * count * height * labels, (4 * count + 4 * slots) * height * labels),
        name="collect",
    )(rows, other_rows, mine, theirs)


def finish_kernel(anchor, first, second, came_first, came_second, state, out, result):
    docs, labels = state.shape
    slots, half = first.shape[:2]
    lane = lax.broadcasted_iota(jnp.int32, (1, labels), 1)
    for slot in range(slots):
        for side, (keep, came) in enumerate(((first, came_first), (second, came_second))):
            here = pl.ds((slot * 2 + side) * half, half)
            total = keep[slot].astype(jnp.float32) + came[slot].astype(jnp.float32)
            total = total + state[here].astype(jnp.float32)
            result[here] = total / jnp.sum(total, axis=-1, keepdims=True)
    count = anchor.shape[0] // 2
    first_row = lax.axis_index(WIDE + ("zl",)) * docs
    for k in range(count):
        row = anchor[k] - first_row
        result[pl.ds(row, 1)] = (lane == anchor[count + k]).astype(jnp.float32)
    out[...] = result[...].astype(out.dtype)


def finish(anchor, keep, came, state):
    docs, labels = state.shape
    return pl.pallas_call(
        finish_kernel,
        out_shape=jax.ShapeDtypeStruct(state.shape, state.dtype),
        in_specs=[SMEM] + [VMEM] * 5,
        out_specs=VMEM,
        scratch_shapes=[pltpu.VMEM((docs, labels), jnp.float32)],
        compiler_params=small(4),
        cost_estimate=cost(6 * docs * labels, 10 * docs * labels),
        name="finish",
    )(anchor, *keep, *came, state)


def local(state, block_values, block_rows, block_cols, anchor_ids, anchor_class):
    doc_dev, labels = state.shape
    width = block_values.shape[2]
    per_dev = doc_dev // width
    values = block_values[:, 0]
    cols = block_cols[:, 0]
    rows = block_rows[:, 0]
    zh, line = lax.axis_index("zh"), lax.axis_index("zl")
    bits = {s: (line >> b) & 1 for b, s in enumerate((1, 2, 4, 8))}

    from_second = lax.ppermute(state, "zh", [(1, 0)])

    def fill(index, buffer, value):
        def gather(buffer, value):
            return plane_exchange(spread(value))

        return lax.cond(zh == index, gather, lambda buffer, value: buffer, buffer, value)

    near_own = fill(0, blank(state), state)
    again, near_own = lax.optimization_barrier((state, near_own))
    from_first = lax.ppermute(again, "zh", [(0, 1)])
    near_own, from_second = lax.optimization_barrier((near_own, from_second))
    near_own = fill(1, near_own, state)
    far = jnp.where(zh == 0, from_second, from_first)
    facts, near_own = lax.optimization_barrier((jnp.concatenate([rows, cols]), near_own))
    other_facts = tuple(exchange(facts, step) for step in (1, 2))
    far_own = plane_exchange(spread(far)).reshape(-1, labels)
    far_own, other_facts = lax.optimization_barrier((far_own, other_facts))
    near_own = near_own.reshape(-1, labels)
    near_other = swap(near_own, "c")
    far_other = swap(far_own, "c")
    mine = products(facts, values, (near_own, near_other, far_own, far_other))

    theirs = [exchange(part, step) for part, step in zip(mine, (1, 2))]
    held = [
        collect(per_dev, order, facts, *parts)
        for order, *parts in zip(((0, 1), (1, 0)), other_facts, mine, theirs)
    ]
    got = [exchange(send, step) for (_, send), step in zip(held, (2, 1))]

    def halve(keep, came, step):
        pair = (2, keep.shape[0] // 2) + keep.shape[1:]
        keep, came = keep.reshape(pair), came.reshape(pair)
        bit = bits[step]

        def at(value, index):
            starts, sizes = (index,) + (0,) * 3, (1,) + value.shape[1:]
            return lax.dynamic_slice(value, starts, sizes, allow_negative_indices=False)[0]

        def side(index):
            one = at(keep, index)
            two = at(came, index)
            return one + two

        return side(bit), side(1 - bit)

    held = [halve(keep, came, 4) for (keep, _), came in zip(held, got)]
    got = [exchange(send, 4) for _, send in held]
    held = [halve(keep, came, 8) for (keep, _), came in zip(held, got)]
    anchor = lax.optimization_barrier(jnp.concatenate([anchor_ids, anchor_class]))
    return finish(anchor, [keep for keep, _ in held], [exchange(send, 8) for _, send in held], state)


def solution(mesh):
    shape = (HALF, SIDE, SIDE, 2, LINE)
    every = WIDE + ("zl",)
    fine = Mesh(mesh.devices.reshape(shape), every)
    in_specs = (
        P(every, None),
        P(WIDE, "zl", None, None),
        P(WIDE, "zl"),
        P(WIDE, "zl"),
        P(every),
        P(every),
    )
    return jax.shard_map(
        local, mesh=fine, in_specs=in_specs, out_specs=P(every, None), check_vma=False
    )
```

```python
import functools

import jax
import jax.numpy as jnp
from jax import lax
from jax.experimental import pallas as pl
from jax.experimental.pallas import tpu as pltpu
from jax.sharding import Mesh, PartitionSpec as P

WIDE = ("zh", "x", "y", "c")
PLANE = ("x", "y")
HALF, SIDE, LINE = 2, 4, 16
FIRST = 3
N_PLANE = SIDE * SIDE
SMEM = pl.BlockSpec(memory_space=pltpu.SMEM)
VMEM = pl.BlockSpec(memory_space=pltpu.VMEM)


def cost(flops, nbytes):
    return pl.CostEstimate(flops=flops, bytes_accessed=nbytes, transcendentals=0)


def swap(value, axis):
    return lax.ppermute(value, axis, [(0, 1), (1, 0)])


def exchange(value, step):
    return lax.ppermute(value, "zl", [(i, i ^ step) for i in range(LINE)])


def spread(value):
    return jnp.broadcast_to(value[None], (N_PLANE,) + value.shape)


def plane_exchange(value):
    return lax.all_to_all(value, PLANE, 0, 0)


def blank_kernel(out):
    pass


def blank(like):
    return pl.pallas_call(
        blank_kernel,
        out_shape=jax.ShapeDtypeStruct((N_PLANE,) + like.shape, like.dtype),
        out_specs=pl.BlockSpec(memory_space=pl.ANY),
        cost_estimate=cost(0, 0),
        name="blank",
    )()


def small(limit):
    return pltpu.CompilerParams(vmem_limit_bytes=limit * 2**20)


def product_kernel(facts, values, s00, s01, s10, s11, first, second, picked):
    count, width = values.shape[:2]
    cut = first.shape[1]
    shift = (s00.shape[0] // width // N_PLANE).bit_length() - 1
    zh, mine = lax.axis_index("zh"), lax.axis_index("c")
    for k in range(count):
        col = facts[count + k]
        device, inner = col >> shift, col & ((1 << shift) - 1)
        core, flat, far = device & 1, (device >> 1) & (N_PLANE - 1), (device >> 1) >> 4
        code = 2 * (far ^ zh) + (core ^ mine)
        start = pl.multiple_of(((flat << shift) + inner) * width, width)
        for number, source in enumerate((s00, s01, s10, s11)):

            @pl.when(code == number)
            def _():
                picked[k] = source[pl.ds(start, width), :]

    for k in range(count):
        out = jnp.dot(values[k], picked[k], preferred_element_type=jnp.float32)
        first[k] = out[:cut].astype(first.dtype)
        second[k] = out[cut:].astype(second.dtype)


def products(facts, values, sources):
    count, width, _ = values.shape
    labels = sources[0].shape[-1]
    cut = width * FIRST // 8
    parts = [(count, rows, labels) for rows in (cut, width - cut)]
    return pl.pallas_call(
        product_kernel,
        out_shape=[jax.ShapeDtypeStruct(part, jnp.bfloat16) for part in parts],
        in_specs=[SMEM] + [VMEM] * 5,
        out_specs=(VMEM, VMEM),
        scratch_shapes=[pltpu.VMEM((count, width, labels), jnp.bfloat16)],
        compiler_params=small(16),
        cost_estimate=cost(2 * count * width * width * labels, 6 * count * width * labels),
        name="products",
    )(facts, values, *sources)


def collect_kernel(per_dev, order, rows, other_rows, mine, theirs, keep, send, total):
    slots = keep.shape[0]
    line = lax.axis_index("zl")
    shift = per_dev.bit_length() - 1
    total[...] = jnp.zeros_like(total)
    for numbers, source in ((rows, mine), (other_rows, theirs)):
        for k in range(source.shape[0]):
            owner, inner = numbers[k] >> shift, numbers[k] & (per_dev - 1)
            pair = ((owner >> 2) & 1) * 2 + (owner >> 3)
            differs = owner ^ line
            goes = (differs >> order[1]) & 1
            place = (pair << shift) + inner + goes * slots

            @pl.when(((differs >> order[0]) & 1) == 0)
            def _():
                total[place] += source[k].astype(jnp.float32)

    send[...] = total[slots:].astype(send.dtype)
    keep[...] = total[:slots].astype(keep.dtype)


def collect(per_dev, order, rows, other_rows, mine, theirs):
    count, height, labels = mine.shape
    slots = LINE // 4 * per_dev
    part = jax.ShapeDtypeStruct((slots, height, labels), jnp.bfloat16)
    return pl.pallas_call(
        functools.partial(collect_kernel, per_dev, order),
        out_shape=(part, part),
        in_specs=[SMEM, SMEM, VMEM, VMEM],
        out_specs=(VMEM, VMEM),
        scratch_shapes=[pltpu.VMEM((2 * slots, height, labels), jnp.float32)],
        compiler_params=small(4),
        cost_estimate=cost(2 * count * height * labels, (4 * count + 4 * slots) * height * labels),
        name="collect",
    )(rows, other_rows, mine, theirs)


def finish_kernel(anchor, first, second, came_first, came_second, state, out, result):
    docs, labels = state.shape
    slots, cut = first.shape[:2]
    width = docs // slots
    lane = lax.broadcasted_iota(jnp.int32, (1, labels), 1)
    for slot in range(slots):
        for side, (keep, came) in enumerate(((first, came_first), (second, came_second))):
            here = pl.ds(slot * width + side * cut, keep.shape[1])
            total = keep[slot].astype(jnp.float32) + came[slot].astype(jnp.float32)
            total = total + state[here].astype(jnp.float32)
            result[here] = total / jnp.sum(total, axis=-1, keepdims=True)
    count = anchor.shape[0] // 2
    first_row = lax.axis_index(WIDE + ("zl",)) * docs
    for k in range(count):
        row = anchor[k] - first_row
        result[pl.ds(row, 1)] = (lane == anchor[count + k]).astype(jnp.float32)
    out[...] = result[...].astype(out.dtype)


def finish(anchor, keep, came, state):
    docs, labels = state.shape
    return pl.pallas_call(
        finish_kernel,
        out_shape=jax.ShapeDtypeStruct(state.shape, state.dtype),
        in_specs=[SMEM] + [VMEM] * 5,
        out_specs=VMEM,
        scratch_shapes=[pltpu.VMEM((docs, labels), jnp.float32)],
        compiler_params=small(4),
        cost_estimate=cost(6 * docs * labels, 10 * docs * labels),
        name="finish",
    )(anchor, *keep, *came, state)


def local(state, block_values, block_rows, block_cols, anchor_ids, anchor_class):
    doc_dev, labels = state.shape
    width = block_values.shape[2]
    per_dev = doc_dev // width
    values = block_values[:, 0]
    cols = block_cols[:, 0]
    rows = block_rows[:, 0]
    zh, line = lax.axis_index("zh"), lax.axis_index("zl")
    bits = {s: (line >> b) & 1 for b, s in enumerate((1, 2, 4, 8))}

    from_second = lax.ppermute(state, "zh", [(1, 0)])

    def fill(index, buffer, value):
        def gather(buffer, value):
            return plane_exchange(spread(value))

        return lax.cond(zh == index, gather, lambda buffer, value: buffer, buffer, value)

    near_own = fill(0, blank(state), state)
    again, near_own = lax.optimization_barrier((state, near_own))
    from_first = lax.ppermute(again, "zh", [(0, 1)])
    near_own, from_second = lax.optimization_barrier((near_own, from_second))
    near_own = fill(1, near_own, state)
    far = jnp.where(zh == 0, from_second, from_first)
    facts, near_own = lax.optimization_barrier((jnp.concatenate([rows, cols]), near_own))
    other_facts = tuple(exchange(facts, step) for step in (1, 2))
    far_own = plane_exchange(spread(far)).reshape(-1, labels)
    far_own, other_facts = lax.optimization_barrier((far_own, other_facts))
    near_own = near_own.reshape(-1, labels)
    near_other = swap(near_own, "c")
    far_other = swap(far_own, "c")
    mine = products(facts, values, (near_own, near_other, far_own, far_other))

    theirs = [exchange(part, step) for part, step in zip(mine, (1, 2))]
    held = [
        collect(per_dev, order, facts, *parts)
        for order, *parts in zip(((0, 1), (1, 0)), other_facts, mine, theirs)
    ]
    got = [exchange(send, step) for (_, send), step in zip(held, (2, 1))]

    def halve(keep, came, step):
        pair = (2, keep.shape[0] // 2) + keep.shape[1:]
        keep, came = keep.reshape(pair), came.reshape(pair)
        bit = bits[step]

        def at(value, index):
            starts, sizes = (index,) + (0,) * 3, (1,) + value.shape[1:]
            return lax.dynamic_slice(value, starts, sizes, allow_negative_indices=False)[0]

        def side(index):
            one = at(keep, index)
            two = at(came, index)
            return one + two

        return side(bit), side(1 - bit)

    held = [halve(keep, came, 4) for (keep, _), came in zip(held, got)]
    got = [exchange(send, 4) for _, send in held]
    held = [halve(keep, came, 8) for (keep, _), came in zip(held, got)]
    anchor = lax.optimization_barrier(jnp.concatenate([anchor_ids, anchor_class]))
    return finish(anchor, [keep for keep, _ in held], [exchange(send, 8) for _, send in held], state)


def solution(mesh):
    shape = (HALF, SIDE, SIDE, 2, LINE)
    every = WIDE + ("zl",)
    fine = Mesh(mesh.devices.reshape(shape), every)
    in_specs = (
        P(every, None),
        P(WIDE, "zl", None, None),
        P(WIDE, "zl"),
        P(WIDE, "zl"),
        P(every),
        P(every),
    )
    return jax.shard_map(
        local, mesh=fine, in_specs=in_specs, out_specs=P(every, None), check_vma=False
    )
```
